256 devices in a mesh: tm: 8 (over z), orb: 4 (over y_hi, core), aux: 8 (over y_lo, x).
Axes of the slice: x: 4, y: 4 (y_hi: 2, y_lo: 2; y = y_hi * 2 + y_lo), z: 8, core: 2. Of those that a mesh axis runs over, the one named last changes fastest.
Arguments:
- three_center: bfloat16 [1024, 6, 4096], P('orb', None, 'aux'), may hold values from -1.5 to 1.5
- block_mask: int32 [16, 6, 32], P('orb', None, 'aux'), may hold values from 0 to 1, as said below
- green_functions: bfloat16 [8, 1024, 1024], P('tm', 'orb'), may hold values from -0.1875 to 0.1875
- time_slot: int32 [4], replicated, may hold values from 0 to 3, each once
- grid_times: float32 [4], replicated, may hold values from 0.3 to 3
- grid_frequencies: float32 [4], replicated, may hold values from 0.3 to 3
- cosine_weights: float32 [4, 4], replicated, may hold values from 0.5 to 1.5
Outputs:
- chi_freq: float32 [4096, 4, 4096], P(('tm', 'orb'), None, 'aux')
The draws below stay inside these ranges and needn't reach their ends.
Inputs may be any that keep to these rules, and one draw needn't show every extreme that they name: `block_mask`: 0 or 1. The share of present blocks may differ from one slice of 512 auxiliary functions to another. `time_slot`: each grid time point stands once.
All inputs are finite; a program needn't handle non-finite values.
Results may differ from the reference program's by a relative error of at most 0.004.
Values may be sent and summed in bfloat16 or wider, within the bound.
A program may use at most 64 MiB of HBM per device.

```python
import math
import jax
import jax.numpy as jnp
from jax import lax

W = 1024
BO = 64
BA = 128
AUX_DEV = 512
NB = 6
AUX = 4096
TIMES = 4
NF = 4


def draw_block_mask(key, part):
    key_level, key_roll = jax.random.split(jax.random.fold_in(key, 11))
    groups = AUX // AUX_DEV
    per_group = AUX_DEV // BA
    exponent = jax.random.randint(key_level, (1, 1, groups, 1), 0, 4)
    threshold = jnp.left_shift(jnp.ones_like(exponent), exponent)
    rolled = jax.random.randint(key_roll, (W // BO, NB, groups, per_group), 0, 8)
    return (rolled < threshold).astype(jnp.int32).reshape(W // BO, NB, AUX // BA)


def block_levels(own_key, extent, pieces, least, largest):
    loudness = 1.0
    for position, shards_of in pieces:
        steps = jax.random.uniform(jax.random.fold_in(jax.random.fold_in(own_key, 6), position), (shards_of,), jnp.float32, least / len(pieces), largest / len(pieces))
        loudness = loudness * jnp.repeat(jnp.exp(steps), extent[position] // shards_of).reshape((-1,) + (1,) * (len(extent) - 1 - position))
    return loudness


def noise(own_key, dims, scale, most, pieces=(), kind=jnp.bfloat16):
    values = jax.random.normal(own_key, dims, jnp.float32) * scale
    if len(pieces) > 0:
        values = block_levels(own_key, dims, pieces, -0.22, 0.18) * values
    return jnp.clip(values, min=-most, max=most).astype(kind)


def setup_inputs(seed: int = 0) -> dict:
    splits = jax.random.split(jax.random.key(seed), 8)
    three_center = noise(splits[0], (W, NB, AUX), 0.25, 1.5, ((0, 4), (2, 8)))
    block_mask = draw_block_mask(jax.random.fold_in(splits[7], 71), 0)
    green_functions = noise(splits[2], (2 * TIMES, W, W), W ** -0.5, 0.1875, ((0, 8), (1, 4)))
    time_slot = jax.random.permutation(splits[3], TIMES).astype(jnp.int32)
    grid_times = jnp.clip(jnp.exp(jax.random.uniform(splits[4], (TIMES,), jnp.float32, math.log(0.3), math.log(3.0))), 0.3, 3.0)
    grid_frequencies = jnp.clip(jnp.exp(jax.random.uniform(splits[5], (NF,), jnp.float32, math.log(0.3), math.log(3.0))), 0.3, 3.0)
    cosine_weights = jnp.clip(jax.random.uniform(splits[6], (NF, TIMES), jnp.float32, 0.5, 1.5), 0.5, 1.5)
    return dict(three_center=three_center, block_mask=block_mask, green_functions=green_functions, time_slot=time_slot, grid_times=grid_times, grid_frequencies=grid_frequencies, cosine_weights=cosine_weights)


def reference(three_center, block_mask, green_functions, time_slot, grid_times, grid_frequencies, cosine_weights):
    spread = jnp.repeat(jnp.repeat(block_mask, BO, axis=0), BA, axis=2).astype(jnp.bfloat16)
    masked = three_center * spread
    flat_rows = masked.reshape(W, NB * AUX)
    cosine_table = cosine_weights * jnp.cos(grid_frequencies[:, None] * grid_times[None, :])
    slot_match = (time_slot[:, None] == jnp.arange(TIMES, dtype=jnp.int32)[None, :]).astype(jnp.float32)
    pair_coefs = jnp.dot(cosine_table, slot_match.T, precision=lax.Precision.HIGHEST)
    result = jnp.zeros((AUX, NF, AUX), jnp.float32)
    contract = (((0,), (0,)), ((), ()))
    for pair_index in range(TIMES):
        virtual = lax.dot_general(green_functions[2 * pair_index], flat_rows, contract, preferred_element_type=jnp.float32)
        virtual = virtual.astype(jnp.bfloat16).reshape(W * NB, AUX)
        occupied = lax.dot_general(green_functions[2 * pair_index + 1], flat_rows, contract, preferred_element_type=jnp.float32)
        occupied = occupied.astype(jnp.bfloat16).reshape(W * NB, AUX)
        cross_term = lax.dot_general(occupied, virtual, contract, preferred_element_type=jnp.float32)
        chi_time = 0.5 * (cross_term + cross_term.T)
        result = result + chi_time.T[:, None, :] * pair_coefs[None, :, pair_index, None]
    return result
```

```python
import jax
import jax.numpy as jnp
from jax import lax
from jax.experimental import pallas as pl
from jax.experimental.pallas import tpu as pltpu
from jax.sharding import PartitionSpec as P

MESH = pl.DeviceIdType.MESH
F32 = jnp.float32
BF16 = jnp.bfloat16

CHILD = (3985, 272, 224, 2192)
DEPTH = (23130, 7146, 58372)
DEEPEST = 5
STEPS = ((1, 0), (0, 1), (-1, 0), (0, -1))


def bit_of(table, place):
    return lax.shift_right_logical(jnp.int32(table), place) & 1


def hops_up(j):
    return 4 if j < 2 else 3


def hops_down(j):
    return 3 if j < 2 else 4


def kernel(
    m_ref, mask_ref, g_ref, w_ref, out_ref,
    mp, mq, mqt, tbuf, gc, es, er, tmy, nt, acc, sbuf, rbuf,
    sib_s, sib_r, g_s, g_r, own_sem, tree_s, tree_r, e_s, e_r, pl_s, pl_r, z_s, z_r, ts_s, ts_r, o_s, o_r,
):
    nb = m_ref.shape[0]
    chunks = 2 * nb
    z = lax.axis_index("tm")
    orb = lax.axis_index("orb")
    aux = lax.axis_index("aux")
    yh, c = orb // 2, orb % 2
    yl, x = aux // 4, aux % 4
    y = 2 * yh + yl

    def dev(dx, dy, dz, core):
        ny = (y + dy) % 4
        return ((z + dz) % 8, (ny // 2) * 2 + core, (ny % 2) * 4 + (x + dx) % 4)

    def remote(src, dst, s, r, where):
        return pltpu.make_async_remote_copy(
            src_ref=src, dst_ref=dst, send_sem=s, recv_sem=r, device_id=where, device_id_type=MESH
        )

    sibling = (z, yh * 2 + 1 - c, aux)
    partner = (z, (1 - yh) * 2 + c, aux)
    zpair = z + 1 - 2 * (z % 2)
    swapped = [(zpair, yl * 2 + core, yh * 4 + x) for core in range(2)]

    barrier = pltpu.get_barrier_semaphore()
    greet = [sibling, partner] + swapped
    greet += [((z + d) % 8, orb, aux) for d in range(1, 8)]
    greet += [(z, orb, (aux + d) % 8) for d in range(1, 8)]
    other_y = (y + 3 + 2 * (y % 2)) % 4
    greet += [(z, (other_y // 2) * 2 + c, (other_y % 2) * 4 + x)]
    for where in greet:
        pl.semaphore_signal(barrier, inc=1, device_id=where, device_id_type=MESH)
    pl.semaphore_wait(barrier, len(greet))

    half_rows = pl.ds(pl.multiple_of((x % 2) * 128, 128), 128)
    g_copies = [remote(g_ref.at[half_rows, :], gc, g_s.at[core], g_r, swapped[core]) for core in range(2)]

    @pl.when(c == x // 2)
    def _():
        for copy in g_copies:
            copy.start()

    def sib_copy(n):
        mine = pl.ds(pl.multiple_of(c * 256, 256), 256)
        return remote(mp.at[n, mine, :], mp.at[n, mine, :], sib_s.at[n], sib_r.at[n], sibling)

    for n in range(nb):
        for b in range(4):
            for ab in range(4):
                present = jnp.full((64, 128), mask_ref[b, n, ab].astype(F32), F32).astype(BF16)
                rows = pl.ds(pl.multiple_of(c * 256 + b * 64, 64), 64)
                mp[n, rows, ab * 128:(ab + 1) * 128] = (
                    m_ref[n, b * 64:(b + 1) * 64, ab * 128:(ab + 1) * 128] * present
                )
        sib_copy(n).start()

    rx = (x + 4 - z % 4) % 4
    depth, child, is_root = [], [], []
    for s in range(2):
        ry = (y + 8 - z // 4 - 2 * s) % 4
        px, py = rx, ry
        for t in range(4):
            place = px * 4 + py
            depth.append(bit_of(DEPTH[0], place) + 2 * bit_of(DEPTH[1], place) + 4 * bit_of(DEPTH[2], place))
            child.append([bit_of(CHILD[(e - t) % 4], place) for e in range(4)])
            px, py = py, (4 - px) % 4
        is_root.append((rx + ry) == 0)
    neighbours = [dev(dx, dy, 0, c) for dx, dy in STEPS]

    def tree_copy(s, t, q, e, root):
        n, qb = q // 2, q % 2
        dst = mq.at[n, qb, pl.ds(s * 512 + t * 128, 128), :]
        if root:
            src = mp.at[n, pl.ds(t * 128, 128), pl.ds(pl.multiple_of((c + 2 * qb) * 128, 128), 128)]
        else:
            src = dst
        return remote(src, dst, tree_s.at[4 * s + t, e, q], tree_r.at[4 * s + t, q], neighbours[e])

    def tree_step(k):
        @pl.when(k < nb)
        def _():
            sib_copy(k).wait_recv()

        for s in range(2):
            @pl.when(is_root[s] & (k < chunks))
            def _(s=s):
                for t in range(4):
                    tree_copy(s, t, k, t, True).start()

            for t in range(4):
                q = k - depth[4 * s + t]

                @pl.when((depth[4 * s + t] > 0) & (q >= 0) & (q < chunks))
                def _(s=s, t=t, q=q):
                    tree_copy(s, t, q, 0, False).wait_recv()
                    for e in range(4):
                        @pl.when(child[4 * s + t][e] == 1)
                        def _(e=e):
                            tree_copy(s, t, q, e, False).start()

    def tree_sends_done(q):
        for s in range(2):
            for t in range(4):
                for e in range(4):
                    @pl.when(child[4 * s + t][e] == 1)
                    def _(s=s, t=t, e=e):
                        tree_copy(s, t, q, e, False).wait_send()

    def e_copy(d):
        to = (z + d) % 8
        return remote(
            es.at[pl.ds(pl.multiple_of(to * 16, 16), 16), :], er.at[z], e_s.at[d - 1], e_r.at[d - 1], (to, orb, aux)
        )

    def plane_copy(d):
        return remote(
            tmy, tbuf.at[:, c, aux, z], pl_s.at[d - 1], pl_r.at[d - 1], (z, orb, (aux + d) % 8)
        )

    def z_copy(j, h, up):
        origin = (z + 8 - h) % 8 if up else (z + h) % 8
        to = (z + 1) % 8 if up else (z + 7) % 8
        way = 0 if up else 1
        piece = tbuf.at[j, c, :, origin]
        return remote(piece, piece, z_s.at[way, j, h], z_r.at[way, j, h], (to, orb, aux))

    def z_event(j, h):
        for up in (True, False):
            if h < (hops_up(j) if up else hops_down(j)):
                if h > 0:
                    z_copy(j, h - 1, up).wait_recv()
                z_copy(j, h, up).start()

    def t_done(j):
        z_copy(j, hops_up(j) - 1, True).wait_recv()
        z_copy(j, hops_down(j) - 1, False).wait_recv()
        remote(tbuf.at[j, c], tbuf.at[j, c], ts_s.at[j], ts_r.at[j], sibling).start()

    def phase_e():
        remote(g_ref.at[half_rows, :], gc, g_s.at[0], g_r, swapped[0]).wait_recv()
        es[...] = lax.dot_general(gc[...], g_ref[...], (((1,), (1,)), ((), ())), preferred_element_type=F32)
        for d in range(1, 8):
            e_copy(d).start()
        er[z] = es[pl.ds(pl.multiple_of(z * 16, 16), 16), :]

    def phase_t():
        for d in range(1, 8):
            e_copy(d).wait_recv()
        for j in range(4):
            total = w_ref[j, 0] * er[0]
            for s in range(1, 8):
                total = total + w_ref[j, s] * er[s]
            tmy[j] = total.astype(BF16)
        for d in range(1, 8):
            plane_copy(d).start()
        tbuf[:, c, aux, z] = tmy[...]

    def phase_plane():
        for d in range(1, 8):
            plane_copy(d).wait_recv()

    def own_copy(n, qb):
        return pltpu.make_async_copy(
            mp.at[n, :, pl.ds(pl.multiple_of((c + 2 * qb) * 128, 128), 128)],
            mq.at[n, qb, pl.ds(pl.multiple_of(yh * 512, 512), 512), :],
            own_sem.at[n, qb],
        )

    at_source = z == aux
    events = sorted(((1.5 * j + h, j, h) for j in range(4) for h in range(4)))
    events = [(j, h) for _, j, h in events]

    pl.loop(0, 4)(tree_step)
    phase_e()
    pl.loop(4, 7)(tree_step)
    phase_t()
    pl.loop(7, 10)(tree_step)
    phase_plane()
    for i in range(10, chunks + DEEPEST):
        tree_step(jnp.int32(i))
        for j, h in events[2 * (i - 10):2 * (i - 9)]:
            z_event(j, h)
    for j, h in events[2 * (chunks + DEEPEST - 10):]:
        z_event(j, h)
    for j in range(4):
        t_done(j)

    @pl.when(at_source)
    def _():
        for n in range(nb):
            for qb in range(2):
                own_copy(n, qb).start()
        for n in range(nb):
            for qb in range(2):
                own_copy(n, qb).wait()

    @pl.loop(0, nb)
    def _(n):
        for qb in range(2):
            mqt[n, qb * 128:(qb + 1) * 128, :] = mq[n, qb].T

    def o_copy(j):
        return remote(sbuf.at[j], rbuf.at[j], o_s.at[j], o_r.at[j], partner)

    for j in range(4):
        remote(tbuf.at[j, c], tbuf.at[j, 1 - c], ts_s.at[j], ts_r.at[j], sibling).wait_recv()

        @pl.loop(0, nb)
        def _(n, j=j):
            for core in range(2):
                nt[:, core * 256:(core + 1) * 256] = jnp.dot(
                    mqt[n], tbuf[j, core].reshape(1024, 256), preferred_element_type=F32
                ).astype(BF16)
            part = jnp.dot(nt[...], mp[n], preferred_element_type=F32).reshape(2, 128, 512)

            @pl.when(n == 0)
            def _():
                acc[...] = part

            @pl.when(n > 0)
            def _():
                acc[...] += part

        sbuf[j] = acc[1 - yh].astype(BF16)
        o_copy(j).start()
        out_ref[j] = acc[yh]
    for j in range(4):
        o_copy(j).wait_recv()
        out_ref[j] += rbuf[j].astype(F32)

    @pl.when(c == x // 2)
    def _():
        for copy in g_copies:
            copy.wait_send()

    pl.loop(0, chunks)(tree_sends_done)
    for n in range(nb):
        sib_copy(n).wait_send()
    for d in range(1, 8):
        e_copy(d).wait_send()
        plane_copy(d).wait_send()
    for j in range(4):
        for h in range(hops_up(j)):
            z_copy(j, h, True).wait_send()
        for h in range(hops_down(j)):
            z_copy(j, h, False).wait_send()
        remote(tbuf.at[j, c], tbuf.at[j, c], ts_s.at[j], ts_r.at[j], sibling).wait_send()
        o_copy(j).wait_send()


def per_device(
    three_center,
    block_mask,
    green_functions,
    time_slot,
    grid_times,
    grid_frequencies,
    cosine_weights,
):
    nbatch = three_center.shape[1]
    time_count = time_slot.shape[0]
    cosine_table = cosine_weights * jnp.cos(grid_frequencies[:, None] * grid_times[None, :])
    slot_match = (time_slot[:, None] == jnp.arange(time_count, dtype=jnp.int32)[None, :]).astype(F32)
    pair_coefs = jnp.dot(cosine_table, slot_match.T, precision=lax.Precision.HIGHEST)
    weights = 0.5 * jnp.repeat(pair_coefs, 2, axis=1)
    by_batch = jnp.transpose(three_center, (1, 0, 2))
    dma = pltpu.SemaphoreType.DMA
    vmem = pl.BlockSpec(memory_space=pltpu.VMEM)
    smem = pl.BlockSpec(memory_space=pltpu.SMEM)
    result = pl.pallas_call(
        kernel,
        name="polarizability",
        out_shape=jax.ShapeDtypeStruct((4, 128, 512), F32),
        in_specs=[vmem, smem, vmem, smem],
        out_specs=vmem,
        scratch_shapes=[
            pltpu.VMEM((nbatch, 512, 512), BF16),
            pltpu.VMEM((nbatch, 2, 1024, 128), BF16),
            pltpu.VMEM((nbatch, 256, 1024), BF16),
            pltpu.VMEM((4, 2, 8, 8, 16, 256), BF16),
            pltpu.VMEM((128, 1024), BF16),
            pltpu.VMEM((128, 256), F32),
            pltpu.VMEM((8, 16, 256), F32),
            pltpu.VMEM((4, 16, 256), BF16),
            pltpu.VMEM((256, 512), BF16),
            pltpu.VMEM((2, 128, 512), F32),
            pltpu.VMEM((4, 128, 512), BF16),
            pltpu.VMEM((4, 128, 512), BF16),
            dma((nbatch,)), dma((nbatch,)),
            dma((2,)), dma,
            dma((nbatch, 2)),
            dma((8, 4, 2 * nbatch)), dma((8, 2 * nbatch)),
            dma((7,)), dma((7,)),
            dma((7,)), dma((7,)),
            dma((2, 4, 4)), dma((2, 4, 4)),
            dma((4,)), dma((4,)),
            dma((4,)), dma((4,)),
        ],
        compiler_params=pltpu.CompilerParams(
            collective_id=0, has_side_effects=True, vmem_limit_bytes=48 * 1024 * 1024
        ),
        cost_estimate=pl.CostEstimate(flops=9_700_000_000, bytes_accessed=3_000_000, transcendentals=0),
    )(by_batch, block_mask, green_functions[0], weights)
    return jnp.transpose(result, (1, 0, 2))


def solution(mesh):
    return jax.shard_map(
        per_device,
        mesh=mesh,
        in_specs=(
            P("orb", None, "aux"),
            P("orb", None, "aux"),
            P("tm", "orb", None),
            P(),
            P(),
            P(),
            P(),
        ),
        out_specs=P(("tm", "orb"), None, "aux"),
        check_vma=False,
    )
```

```python
import jax
import jax.numpy as jnp
from jax import lax
from jax.experimental import pallas as pl
from jax.experimental.pallas import tpu as pltpu
from jax.sharding import PartitionSpec as P

MESH = pl.DeviceIdType.MESH
F32 = jnp.float32
BF16 = jnp.bfloat16
PARTS = 2


def kernel(
    m_ref, mask_ref, g_ref, w_ref, out_ref,
    mp, mq, mqt, sbuf, gc, es, er, smy, nt, acc, own, oout, oin,
    sib_s, sib_r, g_s, g_r, e_s, e_r, sc_s, sc_r, p1_s, p1_r, p2_s, p2_r, pl_s, pl_r, z_s, z_r, t_s, t_r, o_s, o_r,
):
    nb = m_ref.shape[0]
    z = lax.axis_index("tm")
    orb = lax.axis_index("orb")
    aux = lax.axis_index("aux")
    yh, c = orb // 2, orb % 2
    yl, x = aux // 4, aux % 4
    y = 2 * yh + yl

    def dev(to_x, to_y, to_z, core):
        return (to_z, (to_y // 2) * 2 + core, (to_y % 2) * 4 + to_x)

    def remote(src, dst, s, r, where):
        return pltpu.make_async_remote_copy(
            src_ref=src, dst_ref=dst, send_sem=s, recv_sem=r, device_id=where, device_id_type=MESH
        )

    def rows(start, size):
        return pl.ds(pl.multiple_of(start, size), size)

    sibling = (z, yh * 2 + 1 - c, aux)
    partner = (z, (1 - yh) * 2 + c, aux)
    zpair = z + 1 - 2 * (z % 2)
    swapped = [(zpair, yl * 2 + core, yh * 4 + x) for core in range(2)]
    z_next = ((z + 1) % 8, orb, aux)
    z_last = ((z + 7) % 8, orb, aux)
    i = (x + 4 - z % 4) % 4
    el = (y + 4 - z // 4) % 4
    place = el * 4 + i
    x_peers = [dev((x + d) % 4, y, z, c) for d in range(1, 4)]
    y_peers = [dev(x, (y + d) % 4, z, c) for d in range(1, 4)]

    barrier = pltpu.get_barrier_semaphore()
    greet = [sibling] + swapped + x_peers + y_peers + [z_next, z_last]
    greet += [dev((x + d) % 4, yh * 2 + 1 - yl, z, c) for d in range(1, 4)]
    for where in greet:
        pl.semaphore_signal(barrier, inc=1, device_id=where, device_id_type=MESH)
    for d in range(8):
        pl.semaphore_signal(barrier, inc=1, device_id=((z + d) % 8, el, z), device_id_type=MESH)

    for n in range(nb):
        for b in range(4):
            for ab in range(4):
                present = jnp.full((64, 128), mask_ref[b, n, ab].astype(F32), F32).astype(BF16)
                mp[n, rows(c * 256 + b * 64, 64), ab * 128:(ab + 1) * 128] = (
                    m_ref[n, b * 64:(b + 1) * 64, ab * 128:(ab + 1) * 128] * present
                )
    pl.semaphore_wait(barrier, len(greet) + 8)

    half_rows = rows((x % 2) * 128, 128)

    def g_copy(core):
        return remote(g_ref.at[half_rows, :], gc, g_s.at[core], g_r, swapped[core])

    @pl.when(c == x // 2)
    def _():
        for core in range(2):
            g_copy(core).start()

    strip = (z // 2) * 16

    def scatter(step, core):
        src = mp.at[:, rows(c * 256 + step * 64 + strip, 16), rows((core + 2 * (z % 2)) * 128, 128)]
        dst = mq.at[:, z % 2, orb, step, rows(strip, 16), :]
        where = dev((x + step) % 4, (y + c) % 4, aux, core)
        return src, dst, where

    def scatter_all(act):
        for step in range(4):
            for core in range(2):
                src, dst, where = scatter(step, core)
                send = remote(src, dst, sc_s.at[step, core], sc_r.at[z], where)
                if step == 0 and core == 0:
                    to_self = (z == aux) & (c == 0)

                    @pl.when(to_self)
                    def _():
                        if act == "start":
                            pltpu.make_async_copy(src, dst, sc_r.at[z]).start()

                    @pl.when(jnp.logical_not(to_self))
                    def _():
                        if act == "start":
                            send.start()
                        else:
                            send.wait_send()
                elif act == "start":
                    send.start()
                else:
                    send.wait_send()

    scatter_all("start")

    def sib_copy(n):
        mine = rows(c * 256, 256)
        part = pl.ds(n * 3, 3)
        return remote(mp.at[part, mine, :], mp.at[part, mine, :], sib_s.at[n], sib_r.at[n], sibling)

    for n in range(PARTS):
        sib_copy(n).start()

    keep = z % 2

    def e_copy():
        return remote(es.at[1 - keep], er, e_s, e_r, (zpair, orb, aux))

    def plane_copy(d):
        return remote(smy, sbuf.at[z, c, aux], pl_s.at[d - 1], pl_r.at[d - 1], (z, orb, (aux + d) % 8))

    g_copy(0).wait_recv()
    es[...] = (0.5 * lax.dot_general(
        gc[...], g_ref[...], (((1,), (1,)), ((), ())), preferred_element_type=F32
    )).reshape(2, 64, 256)
    e_copy().start()

    def first_copy(part, way, d):
        span = pl.ds(part * 3, 3)
        piece = mq.at[span, way, el, i]
        peer = (x_peers if way == 0 else y_peers)[d]
        return remote(piece, piece, p1_s.at[part, way, d], p1_r.at[part, way, d], peer)

    def second_copy(part, way, d):
        span = pl.ds(part * 3, 3)
        piece = mq.at[span, 0, el] if way == 0 else mq.at[span, 1, :, i]
        peer = (y_peers if way == 0 else x_peers)[d]
        return remote(piece, piece, p2_s.at[part, way, d], p2_r.at[part, way, d], peer)

    for s in range(8):
        src, dst, where = scatter(1, 0)
        remote(src, dst, sc_s.at[1, 0], sc_r.at[s], where).wait_recv()
    for part in range(PARTS):
        for way in range(2):
            for d in range(3):
                first_copy(part, way, d).start()

    e_copy().wait_recv()
    smy[...] = (es[keep] + er[...]).astype(BF16)
    for d in range(1, 8):
        plane_copy(d).start()
    sbuf[z, c, aux] = smy[...]

    for part in range(PARTS):
        for way in range(2):
            for d in range(3):
                first_copy(part, way, d).wait_recv()
            for d in range(3):
                second_copy(part, way, d).start()

    def z_copy(h, half, up):
        origin = (z + 8 - h) % 8 if up else (z + h) % 8
        piece = sbuf.at[origin, c, pl.ds(half * 4, 4)]
        way = 0 if up else 1
        return remote(piece, piece, z_s.at[way, half, h], z_r.at[way, half, h], z_next if up else z_last)

    def hops(half, up):
        return 4 if (half == 0) == up else 3

    def to_sibling(h, half, up):
        origin = (z + 8 - h) % 8 if up else (z + h) % 8
        piece = sbuf.at[origin, c, pl.ds(half * 4, 4)]
        way = 0 if up else 1
        return remote(piece, piece, t_s.at[way, half, h], t_r.at[way, half, h], sibling)

    WAYS = [(half, up) for half in range(2) for up in (True, False)]

    def z_event(h):
        for half, up in WAYS:
            if h <= hops(half, up):
                if h > 0:
                    z_copy(h - 1, half, up).wait_recv()
                if h < hops(half, up):
                    z_copy(h, half, up).start()
                if h > 0 or up:
                    to_sibling(h, half, up).start()

    def sibling_ready(h):
        for half, up in WAYS:
            if h <= hops(half, up) and (h > 0 or up):
                to_sibling(h, half, up).wait_recv()

    for d in range(1, 8):
        plane_copy(d).wait_recv()
    z_event(0)
    z_event(1)
    z_event(2)

    for n in range(PARTS):
        sib_copy(n).wait_recv()
    for part in range(PARTS):
        for way in range(2):
            for d in range(3):
                second_copy(part, way, d).wait_recv()

        @pl.loop(part * 3, part * 3 + 3)
        def _(n):
            for qb in range(2):
                block = mq[n, qb].reshape(8, 2, 64, 128)
                for half in range(2):
                    mqt[n, half, qb * 128:(qb + 1) * 128, :] = block[:, half].reshape(512, 128).T

    turn = 1 - 2 * (z % 2)
    order = [z // 2, (z // 2 + 4 - turn) % 4, (z // 2 + 4 + turn) % 4, (z // 2 + 2) % 4]

    def o_copy(r):
        return remote(oout.at[r], oin.at[r], o_s.at[r], o_r.at[r], partner)

    sibling_ready(0)
    for r in range(4):
        if r >= 2:
            z_event(r + 1)
        sibling_ready(r + 1)

        @pl.loop(0, nb)
        def _(n, r=r):
            for core in range(2):
                nt[:, core * 256:(core + 1) * 256] = (
                    jnp.dot(mqt[n, 0], sbuf[2 * order[r], core].reshape(512, 256), preferred_element_type=F32)
                    + jnp.dot(mqt[n, 1], sbuf[2 * order[r] + 1, core].reshape(512, 256), preferred_element_type=F32)
                ).astype(BF16)
            part = jnp.dot(nt[...], mp[n], preferred_element_type=F32).reshape(2, 128, 512)

            @pl.when(n == 0)
            def _():
                acc[...] = part

            @pl.when(n > 0)
            def _():
                acc[...] += part

        oout[r] = acc[1 - yh].astype(BF16)
        o_copy(r).start()
        own[r] = acc[yh]
    for r in range(4):
        o_copy(r).wait_recv()
        whole = own[r] + oin[r].astype(F32)
        for j in range(4):
            if r == 0:
                out_ref[j] = w_ref[j, order[r]] * whole
            else:
                out_ref[j] += w_ref[j, order[r]] * whole

    @pl.when(c == x // 2)
    def _():
        for core in range(2):
            g_copy(core).wait_send()

    scatter_all("wait")
    for n in range(PARTS):
        sib_copy(n).wait_send()
        for way in range(2):
            for d in range(3):
                first_copy(n, way, d).wait_send()
                second_copy(n, way, d).wait_send()
    e_copy().wait_send()
    for d in range(1, 8):
        plane_copy(d).wait_send()
    for half, up in WAYS:
        for h in range(hops(half, up) + 1):
            if h < hops(half, up):
                z_copy(h, half, up).wait_send()
            if h > 0 or up:
                to_sibling(h, half, up).wait_send()
    for r in range(4):
        o_copy(r).wait_send()


def per_device(
    three_center,
    block_mask,
    green_functions,
    time_slot,
    grid_times,
    grid_frequencies,
    cosine_weights,
):
    nb = three_center.shape[1]
    time_count = time_slot.shape[0]
    cosine_table = cosine_weights * jnp.cos(grid_frequencies[:, None] * grid_times[None, :])
    slot_match = (time_slot[:, None] == jnp.arange(time_count, dtype=jnp.int32)[None, :]).astype(F32)
    pair_coefs = jnp.dot(cosine_table, slot_match.T, precision=lax.Precision.HIGHEST)
    by_batch = jnp.transpose(three_center, (1, 0, 2))
    dma = pltpu.SemaphoreType.DMA
    vmem = pl.BlockSpec(memory_space=pltpu.VMEM)
    smem = pl.BlockSpec(memory_space=pltpu.SMEM)
    result = pl.pallas_call(
        kernel,
        name="polarizability",
        out_shape=jax.ShapeDtypeStruct((4, 128, 512), F32),
        in_specs=[vmem, smem, vmem, smem],
        out_specs=vmem,
        scratch_shapes=[
            pltpu.VMEM((nb, 512, 512), BF16),
            pltpu.VMEM((nb, 2, 4, 4, 64, 128), BF16),
            pltpu.VMEM((nb, 2, 256, 512), BF16),
            pltpu.VMEM((8, 2, 8, 64, 256), BF16),
            pltpu.VMEM((128, 1024), BF16),
            pltpu.VMEM((2, 64, 256), F32),
            pltpu.VMEM((64, 256), F32),
            pltpu.VMEM((64, 256), BF16),
            pltpu.VMEM((256, 512), BF16),
            pltpu.VMEM((2, 128, 512), F32),
            pltpu.VMEM((4, 128, 512), F32),
            pltpu.VMEM((4, 128, 512), BF16),
            pltpu.VMEM((4, 128, 512), BF16),
            dma((PARTS,)), dma((PARTS,)),
            dma((2,)), dma,
            dma, dma,
            dma((4, 2)), dma((8,)),
            dma((PARTS, 2, 3)), dma((PARTS, 2, 3)),
            dma((PARTS, 2, 3)), dma((PARTS, 2, 3)),
            dma((7,)), dma((7,)),
            dma((2, 2, 4)), dma((2, 2, 4)),
            dma((2, 2, 5)), dma((2, 2, 5)),
            dma((4,)), dma((4,)),
        ],
        compiler_params=pltpu.CompilerParams(
            collective_id=0, has_side_effects=True, vmem_limit_bytes=48 * 1024 * 1024
        ),
        cost_estimate=pl.CostEstimate(flops=9_700_000_000, bytes_accessed=3_000_000, transcendentals=0),
    )(by_batch, block_mask, green_functions[0], pair_coefs)
    return jnp.transpose(result, (1, 0, 2))


def solution(mesh):
    return jax.shard_map(
        per_device,
        mesh=mesh,
        in_specs=(
            P("orb", None, "aux"),
            P("orb", None, "aux"),
            P("tm", "orb", None),
            P(),
            P(),
            P(),
            P(),
        ),
        out_specs=P(("tm", "orb"), None, "aux"),
        check_vma=False,
    )
```

```python
import jax
import jax.numpy as jnp
from jax import lax
from jax.experimental import pallas as pl
from jax.experimental.pallas import tpu as pltpu
from jax.sharding import PartitionSpec as P

MESH = pl.DeviceIdType.MESH
F32 = jnp.float32
BF16 = jnp.bfloat16
PARTS = 3


def kernel(
    m_ref, g_ref, mask_ref, slot_ref, time_ref, freq_ref, cw_ref, out_ref,
    m_in, g_in, mp, stage, mq, mqt, sbuf, gc, es, er, smy, nt, own, oout, oin,
    in_sem, sib_s, sib_r, g_s, g_r, e_s, e_r, sp_s, sp_r, sc_s, sc_r, p1_s, p1_r, p2_s, p2_r, pl_s, pl_r, z_s, z_r, t_s, t_r, o_s, o_r,
):
    nb = m_ref.shape[0]
    load_m = pltpu.make_async_copy(m_ref, m_in, in_sem.at[0])
    load_g = pltpu.make_async_copy(g_ref, g_in, in_sem.at[1])
    load_m.start()
    load_g.start()
    z = lax.axis_index("tm")
    orb = lax.axis_index("orb")
    aux = lax.axis_index("aux")
    yh, c = (orb >> 1), (orb & 1)
    yl, x = (aux >> 2), (aux & 3)
    y = 2 * yh + yl

    def dev(to_x, to_y, to_z, core):
        return (to_z, ((to_y >> 1)) * 2 + core, ((to_y & 1)) * 4 + to_x)

    def remote(src, dst, s, r, where):
        return pltpu.make_async_remote_copy(
            src_ref=src, dst_ref=dst, send_sem=s, recv_sem=r, device_id=where, device_id_type=MESH
        )

    def rows(start, size):
        return pl.ds(pl.multiple_of(start, size), size)

    sibling = (z, yh * 2 + 1 - c, aux)
    partner = (z, (1 - yh) * 2 + c, aux)
    zpair = z + 1 - 2 * ((z & 1))
    swapped = [(zpair, yl * 2 + core, yh * 4 + x) for core in range(2)]
    z_next = ((z + 1) & 7, orb, aux)
    z_last = ((z + 7) & 7, orb, aux)
    i = (x + 4 - (z & 3)) & 3
    el = (y + 4 - (z >> 2)) & 3
    place = el * 4 + i
    x_peers = [dev((x + d) & 3, y, z, c) for d in range(1, 4)]
    y_peers = [dev(x, (y + d) & 3, z, c) for d in range(1, 4)]

    barrier = pltpu.get_barrier_semaphore()
    greet = [sibling] + swapped + x_peers + y_peers + [z_next, z_last]
    greet += [dev((x + d) & 3, yh * 2 + 1 - yl, z, c) for d in range(1, 4)]
    greet += [((z + d) & 7, orb, aux) for d in (2, 3, 5, 6)]
    greet += [(z, (y + 4 - (slab >> 2)) & 3, slab) for slab in range(8)]
    for where in greet:
        pl.semaphore_signal(barrier, inc=1, device_id=where, device_id_type=MESH)

    load_m.wait()
    for n in range(nb):
        for b in range(4):
            for ab in range(4):
                present = jnp.full((64, 128), mask_ref[b, ab, n].astype(F32), F32).astype(BF16)
                mp[n, rows(c * 256 + b * 64, 64), ab * 128:(ab + 1) * 128] = (
                    m_in[n, b * 64:(b + 1) * 64, ab * 128:(ab + 1) * 128] * present
                )
    pl.semaphore_wait(barrier, len(greet))

    half_rows = rows(((x & 1)) * 128, 128)

    def g_copy(core):
        return remote(g_ref.at[half_rows, :], gc, g_s.at[core], g_r, swapped[core])

    @pl.when(c == (x >> 1))
    def _():
        for core in range(2):
            g_copy(core).start()

    ahead = (z + 8 - aux) & 7
    batch = jnp.where(ahead == 0, 0, jnp.where(ahead < 4, 2 * ahead - 1, 2 * (8 - ahead)))
    batch = jnp.minimum(batch, nb - 1)

    def spread(step, core, qb):
        src = mp.at[batch, rows(c * 256 + step * 64, 64), rows((core + 2 * qb) * 128, 128)]
        dst = stage.at[ahead, qb]
        where = dev((x + step) & 3, (y + c) & 3, z, core)
        return src, dst, where

    def spread_all(act):
        for qb in range(2):
            sends = (ahead < 3) | (ahead > 5) | ((ahead == 3) if qb == 0 else (ahead == 5))

            @pl.when(sends)
            def _(qb=qb):
                for step in range(4):
                    for core in range(2):
                        src, dst, where = spread(step, core, qb)
                        send = remote(src, dst, sp_s.at[step, core, qb], sp_r.at[ahead, qb], where)

                        def go(send=send):
                            if act == "start":
                                send.start()
                            else:
                                send.wait_send()

                        if step == 0 and core == 0:
                            pl.when(c == 1)(go)
                            if act == "start":
                                @pl.when(c == 0)
                                def _():
                                    pltpu.make_async_copy(src, dst, sp_r.at[ahead, qb]).start()
                        else:
                            go()

    spread_all("start")

    def behind(dz, qb):
        slab = (z + 8 - dz) & 7
        n = 0 if dz == 0 else (2 * dz - 1 if dz < 4 else 2 * (8 - dz))
        n = min(n, nb - 1)
        dst = mq.at[n, qb, (y + 4 - (slab >> 2)) & 3, (x + 4 - (slab & 3)) & 3]
        if dz == 0:
            return pltpu.make_async_copy(stage.at[dz, qb], dst, sc_r.at[n, qb])
        return remote(stage.at[dz, qb], dst, sc_s.at[dz, qb], sc_r.at[n, qb], (slab, orb, aux))

    BLOCKS = [(dz, qb) for dz in (0, 1, 7, 2, 6) for qb in range(2)] + [(3, 0), (5, 1)]

    def pass_on():
        for dz, qb in BLOCKS:
            remote(stage.at[dz, qb], stage.at[dz, qb], sp_s.at[0, 0, qb], sp_r.at[dz, qb], sibling).wait_recv()
            behind(dz, qb).start()

    def sib_copy(n):
        mine = rows(c * 256, 256)
        part = pl.ds(n * 2, 2)
        return remote(mp.at[part, mine, :], mp.at[part, mine, :], sib_s.at[n], sib_r.at[n], sibling)

    for n in range(PARTS):
        sib_copy(n).start()

    keep = (z & 1)

    def e_copy():
        return remote(es.at[1 - keep], er, e_s, e_r, (zpair, orb, aux))

    def plane_copy(d):
        return remote(smy, sbuf.at[z, c, aux], pl_s.at[d - 1], pl_r.at[d - 1], (z, orb, (aux + d) & 7))


    def first_copy(part, way, d):
        span = pl.ds(part * 2, 2)
        piece = mq.at[span, way, el, i]
        peer = (x_peers if way == 0 else y_peers)[d]
        return remote(piece, piece, p1_s.at[part, way, d], p1_r.at[part, way, d], peer)

    def second_copy(part, way, d):
        span = pl.ds(part * 2, 2)
        piece = mq.at[span, 0, el] if way == 0 else mq.at[span, 1, :, i]
        peer = (y_peers if way == 0 else x_peers)[d]
        return remote(piece, piece, p2_s.at[part, way, d], p2_r.at[part, way, d], peer)

    def first(part):
        for n in (2 * part, 2 * part + 1):
            for qb in range(2):
                remote(mq.at[n, qb, 0, 0], mq.at[n, qb, 0, 0], sc_s.at[1, qb], sc_r.at[n, qb], sibling).wait_recv()
        for way in range(2):
            for d in range(3):
                first_copy(part, way, d).start()

    def second(part):
        for way in range(2):
            for d in range(3):
                first_copy(part, way, d).wait_recv()
            for d in range(3):
                second_copy(part, way, d).start()

    def second_done(part):
        for way in range(2):
            for d in range(3):
                second_copy(part, way, d).wait_recv()

        @pl.loop(part * 2, part * 2 + 2)
        def _(n):
            for qb in range(2):
                block = mq[n, qb].reshape(8, 2, 64, 128)
                for half in range(2):
                    mqt[n, qb * 128:(qb + 1) * 128, half * 512:(half + 1) * 512] = (
                        block[:, half].reshape(512, 128).T
                    )

    def z_copy(h, half, up):
        origin = (z + 8 - h) & 7 if up else (z + h) & 7
        piece = sbuf.at[origin, c, pl.ds(half * 4, 4)]
        way = 0 if up else 1
        return remote(piece, piece, z_s.at[way, half, h], z_r.at[way, half, h], z_next if up else z_last)

    def hops(half, up):
        return 4 if (half == 0) == up else 3

    def to_sibling(h, half, up):
        origin = (z + 8 - h) & 7 if up else (z + h) & 7
        piece = sbuf.at[origin, c, pl.ds(half * 4, 4)]
        way = 0 if up else 1
        return remote(piece, piece, t_s.at[way, half, h], t_r.at[way, half, h], sibling)

    WAYS = [(half, up) for half in range(2) for up in (True, False)]

    def z_event(h):
        for half, up in WAYS:
            if h <= hops(half, up):
                if h > 0:
                    z_copy(h - 1, half, up).wait_recv()
                if h < hops(half, up):
                    z_copy(h, half, up).start()
                if h > 0 or up:
                    to_sibling(h, half, up).start()

    def sibling_ready(h):
        for half, up in WAYS:
            if h <= hops(half, up) and (h > 0 or up):
                to_sibling(h, half, up).wait_recv()

    turn = 1 - 2 * ((z & 1))
    order = [(z >> 1), ((z >> 1) + 4 - turn) & 3, ((z >> 1) + 4 + turn) & 3, ((z >> 1) + 2) & 3]

    def o_copy(r, side):
        return remote(oout.at[r, side], oin.at[r, side], o_s.at[r, side], o_r.at[r, side], partner)

    def product(r, part):
        batches = slice(part * 2, part * 2 + 2)
        left = mqt[batches].reshape(512, 1024)
        for core in range(2):
            pair = sbuf[pl.ds(2 * order[r], 2), core].reshape(1024, 256)
            nt[:, :, core * 256:(core + 1) * 256] = (
                jnp.dot(left, pair, preferred_element_type=F32).astype(BF16).reshape(2, 256, 256)
            )
        for side in range(2):
            cols = slice(side * 256, (side + 1) * 256)
            total = jnp.dot(nt[0], mp[part * 2, :, cols], preferred_element_type=F32)
            total += jnp.dot(nt[1], mp[part * 2 + 1, :, cols], preferred_element_type=F32)
            total = total.reshape(2, 128, 256)
            if part > 0:
                total += own[r, side]
            own[r, side] = total
            if part == PARTS - 1:
                oout[r, side] = own[r, side, 1 - yh].astype(BF16)
                o_copy(r, side).start()

    def coefs(r):
        slot = slot_ref[order[r]]
        picked = []
        for j in range(4):
            total = jnp.zeros((8, 256), F32)
            for s in range(4):
                total = total + jnp.where(slot == s, table[j][s], 0.0)
            picked.append(total)
        return picked

    def add(r):
        picked = coefs(r)
        for side in range(2):
            o_copy(r, side).wait_recv()
            whole = (own[r, side, yh] + oin[r, side].astype(F32)).reshape(16, 8, 256)
            cols = slice(side * 256, (side + 1) * 256)
            for j in range(4):
                term = (picked[j] * whole).reshape(128, 256)
                if r == 0:
                    out_ref[j, :, cols] = term
                else:
                    out_ref[j, :, cols] += term

    pass_on()
    load_g.wait()
    g_copy(0).wait_recv()
    es[...] = (0.5 * lax.dot_general(
        gc[...], g_in[...], (((1,), (1,)), ((), ())), preferred_element_type=F32
    )).reshape(2, 64, 256)
    e_copy().start()

    e_copy().wait_recv()
    smy[...] = (es[keep] + er[...]).astype(BF16)
    for d in range(1, 8):
        plane_copy(d).start()
    sbuf[z, c, aux] = smy[...]
    table = [
        [cw_ref[j, s] * jnp.cos(jnp.full((8, 256), freq_ref[j] * time_ref[s], F32)) for s in range(4)]
        for j in range(4)
    ]
    first(0)
    first(1)
    first(2)
    for d in range(1, 8):
        plane_copy(d).wait_recv()
    z_event(0)
    second(0)
    z_event(1)
    second(1)
    second(2)
    for n in range(PARTS):
        sib_copy(n).wait_recv()
    z_event(2)
    sibling_ready(0)
    sibling_ready(1)
    second_done(0)
    product(0, 0)
    sibling_ready(2)
    product(1, 0)
    z_event(3)
    second_done(1)
    product(0, 1)
    product(1, 1)
    sibling_ready(3)
    product(2, 0)
    product(2, 1)
    z_event(4)
    sibling_ready(4)
    product(3, 0)
    product(3, 1)
    second_done(2)
    for r in range(4):
        product(r, 2)
    for r in range(4):
        add(r)

    @pl.when(c == (x >> 1))
    def _():
        for core in range(2):
            g_copy(core).wait_send()

    spread_all("wait")
    for dz, qb in BLOCKS:
        if dz > 0:
            behind(dz, qb).wait_send()
    for n in range(PARTS):
        sib_copy(n).wait_send()
        for way in range(2):
            for d in range(3):
                first_copy(n, way, d).wait_send()
                second_copy(n, way, d).wait_send()
    e_copy().wait_send()
    for d in range(1, 8):
        plane_copy(d).wait_send()
    for half, up in WAYS:
        for h in range(hops(half, up) + 1):
            if h < hops(half, up):
                z_copy(h, half, up).wait_send()
            if h > 0 or up:
                to_sibling(h, half, up).wait_send()
    for r in range(4):
        for side in range(2):
            o_copy(r, side).wait_send()


def per_device(
    three_center,
    block_mask,
    green_functions,
    time_slot,
    grid_times,
    grid_frequencies,
    cosine_weights,
):
    nb = three_center.shape[1]
    by_batch = jnp.transpose(three_center, (1, 0, 2))
    dma = pltpu.SemaphoreType.DMA
    vmem = pl.BlockSpec(memory_space=pltpu.VMEM)
    smem = pl.BlockSpec(memory_space=pltpu.SMEM)
    hbm = pl.BlockSpec(memory_space=pl.ANY)
    result = pl.pallas_call(
        kernel,
        name="polarizability",
        out_shape=jax.ShapeDtypeStruct((4, 128, 512), F32),
        in_specs=[hbm, hbm, smem, smem, smem, smem, smem],
        out_specs=vmem,
        scratch_shapes=[
            pltpu.VMEM((nb, 256, 512), BF16),
            pltpu.VMEM((256, 1024), BF16),
            pltpu.VMEM((nb, 512, 512), BF16),
            pltpu.VMEM((8, 2, 64, 128), BF16),
            pltpu.VMEM((nb, 2, 4, 4, 64, 128), BF16),
            pltpu.VMEM((nb, 256, 1024), BF16),
            pltpu.VMEM((8, 2, 8, 64, 256), BF16),
            pltpu.VMEM((128, 1024), BF16),
            pltpu.VMEM((2, 64, 256), F32),
            pltpu.VMEM((64, 256), F32),
            pltpu.VMEM((64, 256), BF16),
            pltpu.VMEM((2, 256, 512), BF16),
            pltpu.VMEM((4, 2, 2, 128, 256), F32),
            pltpu.VMEM((4, 2, 128, 256), BF16),
            pltpu.VMEM((4, 2, 128, 256), BF16),
            dma((2,)),
            dma((PARTS,)), dma((PARTS,)),
            dma((2,)), dma,
            dma, dma,
            dma((4, 2, 2)), dma((8, 2)),
            dma((8, 2)), dma((nb, 2)),
            dma((PARTS, 2, 3)), dma((PARTS, 2, 3)),
            dma((PARTS, 2, 3)), dma((PARTS, 2, 3)),
            dma((7,)), dma((7,)),
            dma((2, 2, 4)), dma((2, 2, 4)),
            dma((2, 2, 5)), dma((2, 2, 5)),
            dma((4, 2)), dma((4, 2)),
        ],
        compiler_params=pltpu.CompilerParams(
            collective_id=0, has_side_effects=True, vmem_limit_bytes=60 * 1024 * 1024
        ),
        cost_estimate=pl.CostEstimate(flops=9_700_000_000, bytes_accessed=3_000_000, transcendentals=0),
    )(
        by_batch, green_functions[0], jnp.transpose(block_mask, (0, 2, 1)),
        time_slot, grid_times, grid_frequencies, cosine_weights,
    )
    return jnp.transpose(result, (1, 0, 2))


def solution(mesh):
    return jax.shard_map(
        per_device,
        mesh=mesh,
        in_specs=(
            P("orb", None, "aux"),
            P("orb", None, "aux"),
            P("tm", "orb", None),
            P(),
            P(),
            P(),
            P(),
        ),
        out_specs=P(("tm", "orb"), None, "aux"),
        check_vma=False,
    )
```

```python
import jax
import jax.numpy as jnp
from jax import lax
from jax.experimental import pallas as pl
from jax.experimental.pallas import tpu as pltpu
from jax.sharding import PartitionSpec as P

MESH = pl.DeviceIdType.MESH
F32 = jnp.float32
BF16 = jnp.bfloat16
PARTS = 3


def kernel(
    m_ref, g_ref, mask_ref, slot_ref, time_ref, freq_ref, cw_ref, out_ref,
    m_in, g_in, mp, stage, mq, mqt, sbuf, gc, es, er, smy, nt, own, oout, oin,
    in_sem, sib_s, sib_r, g_s, g_r, e_s, e_r, sp_s, sp_r, sc_s, sc_r, p1_s, p1_r, p2_s, p2_r, pl_s, pl_r, z_s, z_r, t_s, t_r, o_s, o_r,
):
    nb = m_ref.shape[0]
    load_m = pltpu.make_async_copy(m_ref, m_in, in_sem.at[0])
    load_g = pltpu.make_async_copy(g_ref, g_in, in_sem.at[1])
    load_m.start()
    load_g.start()
    z = lax.axis_index("tm")
    orb = lax.axis_index("orb")
    aux = lax.axis_index("aux")
    yh, c = (orb >> 1), (orb & 1)
    yl, x = (aux >> 2), (aux & 3)
    y = 2 * yh + yl

    def dev(to_x, to_y, to_z, core):
        return (to_z, ((to_y >> 1)) * 2 + core, ((to_y & 1)) * 4 + to_x)

    def remote(src, dst, s, r, where):
        return pltpu.make_async_remote_copy(
            src_ref=src, dst_ref=dst, send_sem=s, recv_sem=r, device_id=where, device_id_type=MESH
        )

    def rows(start, size):
        return pl.ds(pl.multiple_of(start, size), size)

    sibling = (z, yh * 2 + 1 - c, aux)
    partner = (z, (1 - yh) * 2 + c, aux)
    zpair = z + 1 - 2 * ((z & 1))
    swapped = [(zpair, yl * 2 + core, yh * 4 + x) for core in range(2)]
    z_next = ((z + 1) & 7, orb, aux)
    z_last = ((z + 7) & 7, orb, aux)
    i = (x + 4 - (z & 3)) & 3
    el = (y + 4 - (z >> 2)) & 3
    place = el * 4 + i
    x_peers = [dev((x + d) & 3, y, z, c) for d in range(1, 4)]
    y_peers = [dev(x, (y + d) & 3, z, c) for d in range(1, 4)]

    barrier = pltpu.get_barrier_semaphore()
    greet = [sibling] + swapped + x_peers + y_peers + [z_next, z_last]
    greet += [dev((x + d) & 3, yh * 2 + 1 - yl, z, c) for d in range(1, 4)]
    greet += [((z + d) & 7, orb, aux) for d in (2, 3, 5, 6)]
    greet += [(z, (y + 4 - (slab >> 2)) & 3, slab) for slab in range(8)]
    for where in greet[::-1]:
        pl.semaphore_signal(barrier, inc=1, device_id=where, device_id_type=MESH)

    load_m.wait()
    for n in range(nb):
        for b in range(4):
            for ab in range(4):
                present = jnp.full((64, 128), mask_ref[b, ab, n].astype(F32), F32).astype(BF16)
                mp[n, rows(c * 256 + b * 64, 64), ab * 128:(ab + 1) * 128] = (
                    m_in[n, b * 64:(b + 1) * 64, ab * 128:(ab + 1) * 128] * present
                )
    pl.semaphore_wait(barrier, len(greet))

    half_rows = rows(((x & 1)) * 128, 128)

    def g_copy(core):
        return remote(g_ref.at[half_rows, :], gc, g_s.at[core], g_r, swapped[core])

    @pl.when(c == (x >> 1))
    def _():
        for core in range(2):
            g_copy(core).start()

    ahead = (z + 8 - aux) & 7
    batch = jnp.where(ahead == 0, 0, jnp.where(ahead < 4, 2 * ahead - 1, 2 * (8 - ahead)))
    batch = jnp.minimum(batch, nb - 1)

    def spread(step, core, qb):
        src = mp.at[batch, rows(c * 256 + step * 64, 64), rows((core + 2 * qb) * 128, 128)]
        dst = stage.at[ahead, qb]
        where = dev((x + step) & 3, (y + c) & 3, z, core)
        return src, dst, where

    def spread_all(act):
        for qb in range(2):
            sends = (ahead < 3) | (ahead > 5) | ((ahead == 3) if qb == 0 else (ahead == 5))

            @pl.when(sends)
            def _(qb=qb):
                for step in range(4):
                    for core in range(2):
                        src, dst, where = spread(step, core, qb)
                        send = remote(src, dst, sp_s.at[step, core, qb], sp_r.at[ahead, qb], where)

                        def go(send=send):
                            if act == "start":
                                send.start()
                            else:
                                send.wait_send()

                        if step == 0 and core == 0:
                            pl.when(c == 1)(go)
                            if act == "start":
                                @pl.when(c == 0)
                                def _():
                                    pltpu.make_async_copy(src, dst, sp_r.at[ahead, qb]).start()
                        else:
                            go()

    spread_all("start")

    def behind(dz, qb):
        slab = (z + 8 - dz) & 7
        n = 0 if dz == 0 else (2 * dz - 1 if dz < 4 else 2 * (8 - dz))
        n = min(n, nb - 1)
        dst = mq.at[n, qb, (y + 4 - (slab >> 2)) & 3, (x + 4 - (slab & 3)) & 3]
        if dz == 0:
            return pltpu.make_async_copy(stage.at[dz, qb], dst, sc_r.at[n, qb])
        return remote(stage.at[dz, qb], dst, sc_s.at[dz, qb], sc_r.at[n, qb], (slab, orb, aux))

    BLOCKS = [(dz, qb) for dz in (0, 1, 7, 2, 6) for qb in range(2)] + [(3, 0), (5, 1)]

    def pass_on():
        for dz, qb in BLOCKS:
            remote(stage.at[dz, qb], stage.at[dz, qb], sp_s.at[0, 0, qb], sp_r.at[dz, qb], sibling).wait_recv()
            behind(dz, qb).start()

    def sib_copy(n):
        mine = rows(c * 256, 256)
        part = pl.ds(n * 2, 2)
        return remote(mp.at[part, mine, :], mp.at[part, mine, :], sib_s.at[n], sib_r.at[n], sibling)

    for n in range(PARTS):
        sib_copy(n).start()

    keep = (z & 1)

    def e_copy():
        return remote(es.at[1 - keep], er, e_s, e_r, (zpair, orb, aux))

    def plane_copy(d):
        return remote(smy, sbuf.at[z, c, aux], pl_s.at[d - 1], pl_r.at[d - 1], (z, orb, (aux + d) & 7))


    def first_copy(part, way, d):
        span = pl.ds(part * 2, 2)
        piece = mq.at[span, way, el, i]
        peer = (x_peers if way == 0 else y_peers)[d]
        return remote(piece, piece, p1_s.at[part, way, d], p1_r.at[part, way, d], peer)

    def second_copy(part, way, d):
        span = pl.ds(part * 2, 2)
        piece = mq.at[span, 0, el] if way == 0 else mq.at[span, 1, :, i]
        peer = (y_peers if way == 0 else x_peers)[d]
        return remote(piece, piece, p2_s.at[part, way, d], p2_r.at[part, way, d], peer)

    def first(part):
        for n in (2 * part, 2 * part + 1):
            for qb in range(2):
                remote(mq.at[n, qb, 0, 0], mq.at[n, qb, 0, 0], sc_s.at[1, qb], sc_r.at[n, qb], sibling).wait_recv()
        for way in range(2):
            for d in range(3):
                first_copy(part, way, d).start()

    def second(part):
        for way in range(2):
            for d in range(3):
                first_copy(part, way, d).wait_recv()
            for d in range(3):
                second_copy(part, way, d).start()

    def second_done(part):
        for way in range(2):
            for d in range(3):
                second_copy(part, way, d).wait_recv()

        @pl.loop(part * 2, part * 2 + 2)
        def _(n):
            for qb in range(2):
                block = mq[n, qb].reshape(8, 2, 64, 128)
                for half in range(2):
                    mqt[n, qb * 128:(qb + 1) * 128, half * 512:(half + 1) * 512] = (
                        block[:, half].reshape(512, 128).T
                    )

    def z_copy(h, half, up):
        origin = (z + 8 - h) & 7 if up else (z + h) & 7
        piece = sbuf.at[origin, c, pl.ds(half * 4, 4)]
        way = 0 if up else 1
        return remote(piece, piece, z_s.at[way, half, h], z_r.at[way, half, h], z_next if up else z_last)

    def hops(half, up):
        return 4 if (half == 0) == up else 3

    def to_sibling(h, half, up):
        origin = (z + 8 - h) & 7 if up else (z + h) & 7
        piece = sbuf.at[origin, c, pl.ds(half * 4, 4)]
        way = 0 if up else 1
        return remote(piece, piece, t_s.at[way, half, h], t_r.at[way, half, h], sibling)

    WAYS = [(half, up) for half in range(2) for up in (True, False)]

    def z_event(h):
        for half, up in WAYS:
            if h <= hops(half, up):
                if h > 0:
                    z_copy(h - 1, half, up).wait_recv()
                if h < hops(half, up):
                    z_copy(h, half, up).start()
                if h > 0 or up:
                    to_sibling(h, half, up).start()

    def sibling_ready(h):
        for half, up in WAYS:
            if h <= hops(half, up) and (h > 0 or up):
                to_sibling(h, half, up).wait_recv()

    turn = 1 - 2 * ((z & 1))
    order = [(z >> 1), ((z >> 1) + 4 - turn) & 3, ((z >> 1) + 4 + turn) & 3, ((z >> 1) + 2) & 3]

    def o_copy(r, side):
        return remote(oout.at[r, side], oin.at[r, side], o_s.at[r, side], o_r.at[r, side], partner)

    def product(r, part):
        batches = slice(part * 2, part * 2 + 2)
        left = mqt[batches].reshape(512, 1024)
        for core in range(2):
            pair = sbuf[pl.ds(2 * order[r], 2), core].reshape(1024, 256)
            nt[:, :, core * 256:(core + 1) * 256] = (
                jnp.dot(left, pair, preferred_element_type=F32).astype(BF16).reshape(2, 256, 256)
            )
        for side in range(2):
            cols = slice(side * 256, (side + 1) * 256)
            total = jnp.dot(nt[0], mp[part * 2, :, cols], preferred_element_type=F32)
            total += jnp.dot(nt[1], mp[part * 2 + 1, :, cols], preferred_element_type=F32)
            total = total.reshape(2, 128, 256)
            if part > 0:
                total += own[r, side]
            own[r, side] = total
            if part == PARTS - 1:
                oout[r, side] = own[r, side, 1 - yh].astype(BF16)
                o_copy(r, side).start()

    def coefs(r):
        slot = slot_ref[order[r]]
        picked = []
        for j in range(4):
            total = jnp.zeros((8, 256), F32)
            for s in range(4):
                total = total + jnp.where(slot == s, table[j][s], 0.0)
            picked.append(total)
        return picked

    def add(r):
        picked = coefs(r)
        for side in range(2):
            o_copy(r, side).wait_recv()
            whole = (own[r, side, yh] + oin[r, side].astype(F32)).reshape(16, 8, 256)
            cols = slice(side * 256, (side + 1) * 256)
            for j in range(4):
                term = (picked[j] * whole).reshape(128, 256)
                if r == 0:
                    out_ref[j, :, cols] = term
                else:
                    out_ref[j, :, cols] += term

    load_g.wait()
    g_copy(0).wait_recv()
    es[...] = (0.5 * lax.dot_general(
        gc[...], g_in[...], (((1,), (1,)), ((), ())), preferred_element_type=F32
    )).reshape(2, 64, 256)
    e_copy().start()
    pass_on()

    e_copy().wait_recv()
    smy[...] = (es[keep] + er[...]).astype(BF16)
    for d in range(1, 8):
        plane_copy(d).start()
    sbuf[z, c, aux] = smy[...]
    for d in range(1, 8):
        plane_copy(d).wait_recv()
    z_event(0)
    first(0)
    first(1)
    first(2)
    second(0)
    z_event(1)
    second(1)
    second(2)
    table = [
        [cw_ref[j, s] * jnp.cos(jnp.full((8, 256), freq_ref[j] * time_ref[s], F32)) for s in range(4)]
        for j in range(4)
    ]
    for n in range(PARTS):
        sib_copy(n).wait_recv()
    z_event(2)
    sibling_ready(0)
    sibling_ready(1)
    second_done(0)
    product(0, 0)
    sibling_ready(2)
    product(1, 0)
    z_event(3)
    second_done(1)
    product(0, 1)
    product(1, 1)
    sibling_ready(3)
    product(2, 0)
    product(2, 1)
    z_event(4)
    sibling_ready(4)
    product(3, 0)
    product(3, 1)
    second_done(2)
    for r in range(4):
        product(r, 2)
    for r in range(4):
        add(r)

    @pl.when(c == (x >> 1))
    def _():
        for core in range(2):
            g_copy(core).wait_send()

    spread_all("wait")
    for dz, qb in BLOCKS:
        if dz > 0:
            behind(dz, qb).wait_send()
    for n in range(PARTS):
        sib_copy(n).wait_send()
        for way in range(2):
            for d in range(3):
                first_copy(n, way, d).wait_send()
                second_copy(n, way, d).wait_send()
    e_copy().wait_send()
    for d in range(1, 8):
        plane_copy(d).wait_send()
    for half, up in WAYS:
        for h in range(hops(half, up) + 1):
            if h < hops(half, up):
                z_copy(h, half, up).wait_send()
            if h > 0 or up:
                to_sibling(h, half, up).wait_send()
    for r in range(4):
        for side in range(2):
            o_copy(r, side).wait_send()


def per_device(
    three_center,
    block_mask,
    green_functions,
    time_slot,
    grid_times,
    grid_frequencies,
    cosine_weights,
):
    nb = three_center.shape[1]
    by_batch = jnp.transpose(three_center, (1, 0, 2))
    dma = pltpu.SemaphoreType.DMA
    vmem = pl.BlockSpec(memory_space=pltpu.VMEM)
    smem = pl.BlockSpec(memory_space=pltpu.SMEM)
    hbm = pl.BlockSpec(memory_space=pl.ANY)
    result = pl.pallas_call(
        kernel,
        name="polarizability",
        out_shape=jax.ShapeDtypeStruct((4, 128, 512), F32),
        in_specs=[hbm, hbm, smem, smem, smem, smem, smem],
        out_specs=vmem,
        scratch_shapes=[
            pltpu.VMEM((nb, 256, 512), BF16),
            pltpu.VMEM((256, 1024), BF16),
            pltpu.VMEM((nb, 512, 512), BF16),
            pltpu.VMEM((8, 2, 64, 128), BF16),
            pltpu.VMEM((nb, 2, 4, 4, 64, 128), BF16),
            pltpu.VMEM((nb, 256, 1024), BF16),
            pltpu.VMEM((8, 2, 8, 64, 256), BF16),
            pltpu.VMEM((128, 1024), BF16),
            pltpu.VMEM((2, 64, 256), F32),
            pltpu.VMEM((64, 256), F32),
            pltpu.VMEM((64, 256), BF16),
            pltpu.VMEM((2, 256, 512), BF16),
            pltpu.VMEM((4, 2, 2, 128, 256), F32),
            pltpu.VMEM((4, 2, 128, 256), BF16),
            pltpu.VMEM((4, 2, 128, 256), BF16),
            dma((2,)),
            dma((PARTS,)), dma((PARTS,)),
            dma((2,)), dma,
            dma, dma,
            dma((4, 2, 2)), dma((8, 2)),
            dma((8, 2)), dma((nb, 2)),
            dma((PARTS, 2, 3)), dma((PARTS, 2, 3)),
            dma((PARTS, 2, 3)), dma((PARTS, 2, 3)),
            dma((7,)), dma((7,)),
            dma((2, 2, 4)), dma((2, 2, 4)),
            dma((2, 2, 5)), dma((2, 2, 5)),
            dma((4, 2)), dma((4, 2)),
        ],
        compiler_params=pltpu.CompilerParams(
            collective_id=0, has_side_effects=True, vmem_limit_bytes=60 * 1024 * 1024
        ),
        cost_estimate=pl.CostEstimate(flops=9_700_000_000, bytes_accessed=3_000_000, transcendentals=0),
    )(
        by_batch, green_functions[0], jnp.transpose(block_mask, (0, 2, 1)),
        time_slot, grid_times, grid_frequencies, cosine_weights,
    )
    return jnp.transpose(result, (1, 0, 2))


def solution(mesh):
    return jax.shard_map(
        per_device,
        mesh=mesh,
        in_specs=(
            P("orb", None, "aux"),
            P("orb", None, "aux"),
            P("tm", "orb", None),
            P(),
            P(),
            P(),
            P(),
        ),
        out_specs=P(("tm", "orb"), None, "aux"),
        check_vma=False,
    )
```

```python
import jax
import jax.numpy as jnp
from jax import lax
from jax.experimental import pallas as pl
from jax.experimental.pallas import tpu as pltpu
from jax.sharding import PartitionSpec as P

MESH = pl.DeviceIdType.MESH
F32 = jnp.float32
BF16 = jnp.bfloat16
PARTS = 3


def kernel(
    m_ref, g_ref, mask_ref, slot_ref, time_ref, freq_ref, cw_ref, out_ref,
    m_in, g_in, mp, stage, mq, mqt, sbuf, gc, es, er, smy, nt, own, oout, oin,
    in_sem, sib_s, sib_r, g_s, g_r, e_s, e_r, sp_s, sp_r, sc_s, sc_r, p1_s, p1_r, p2_s, p2_r, pl_s, pl_r, z_s, z_r, t_s, t_r, o_s, o_r,
):
    nb = m_ref.shape[0]
    load_m = pltpu.make_async_copy(m_ref, m_in, in_sem.at[0])
    load_g = pltpu.make_async_copy(g_ref, g_in, in_sem.at[1])
    load_m.start()
    load_g.start()
    z = lax.axis_index("tm")
    orb = lax.axis_index("orb")
    aux = lax.axis_index("aux")
    yh, c = (orb >> 1), (orb & 1)
    yl, x = (aux >> 2), (aux & 3)
    y = 2 * yh + yl

    def dev(to_x, to_y, to_z, core):
        return (to_z, ((to_y >> 1)) * 2 + core, ((to_y & 1)) * 4 + to_x)

    def remote(src, dst, s, r, where):
        return pltpu.make_async_remote_copy(
            src_ref=src, dst_ref=dst, send_sem=s, recv_sem=r, device_id=where, device_id_type=MESH
        )

    def rows(start, size):
        return pl.ds(pl.multiple_of(start, size), size)

    sibling = (z, yh * 2 + 1 - c, aux)
    partner = (z, (1 - yh) * 2 + c, aux)
    zpair = z + 1 - 2 * ((z & 1))
    swapped = [(zpair, yl * 2 + core, yh * 4 + x) for core in range(2)]
    z_next = ((z + 1) & 7, orb, aux)
    z_last = ((z + 7) & 7, orb, aux)
    i = (x + 4 - (z & 3)) & 3
    el = (y + 4 - (z >> 2)) & 3
    place = el * 4 + i
    x_peers = [dev((x + d) & 3, y, z, c) for d in range(1, 4)]
    y_peers = [dev(x, (y + d) & 3, z, c) for d in range(1, 4)]

    barrier = pltpu.get_barrier_semaphore()
    greet = [sibling] + swapped + x_peers + y_peers + [z_next, z_last]
    greet += [dev((x + d) & 3, yh * 2 + 1 - yl, z, c) for d in range(1, 4)]
    greet += [((z + d) & 7, orb, aux) for d in (2, 3, 5, 6)]
    greet += [(z, (y + 4 - (slab >> 2)) & 3, slab) for slab in range(8)]
    for where in greet[::-1]:
        pl.semaphore_signal(barrier, inc=1, device_id=where, device_id_type=MESH)

    load_m.wait()
    for n in range(nb):
        for b in range(4):
            for ab in range(4):
                present = jnp.full((64, 128), mask_ref[b, ab, n].astype(F32), F32).astype(BF16)
                mp[n, rows(c * 256 + b * 64, 64), ab * 128:(ab + 1) * 128] = (
                    m_in[n, b * 64:(b + 1) * 64, ab * 128:(ab + 1) * 128] * present
                )
    pl.semaphore_wait(barrier, len(greet))

    half_rows = rows(((x & 1)) * 128, 128)

    def g_copy(core):
        return remote(g_ref.at[half_rows, :], gc, g_s.at[core], g_r, swapped[core])

    @pl.when(c == (x >> 1))
    def _():
        for core in range(2):
            g_copy(core).start()

    ahead = (z + 8 - aux) & 7
    batch = jnp.where(ahead == 0, 0, jnp.where(ahead < 4, 2 * ahead - 1, 2 * (8 - ahead)))
    batch = jnp.minimum(batch, nb - 1)

    def spread(step, core, qb):
        src = mp.at[batch, rows(c * 256 + step * 64, 64), rows((core + 2 * qb) * 128, 128)]
        dst = stage.at[ahead, qb]
        where = dev((x + step) & 3, (y + c) & 3, z, core)
        return src, dst, where

    def spread_all(act):
        for qb in range(2):
            sends = (ahead < 3) | (ahead > 5) | ((ahead == 3) if qb == 0 else (ahead == 5))

            @pl.when(sends)
            def _(qb=qb):
                for step in range(4):
                    for core in range(2):
                        src, dst, where = spread(step, core, qb)
                        send = remote(src, dst, sp_s.at[step, core, qb], sp_r.at[ahead, qb], where)

                        def go(send=send):
                            if act == "start":
                                send.start()
                            else:
                                send.wait_send()

                        if step == 0 and core == 0:
                            pl.when(c == 1)(go)
                            if act == "start":
                                @pl.when(c == 0)
                                def _():
                                    pltpu.make_async_copy(src, dst, sp_r.at[ahead, qb]).start()
                        else:
                            go()

    spread_all("start")

    def behind(dz, qb):
        slab = (z + 8 - dz) & 7
        n = 0 if dz == 0 else (2 * dz - 1 if dz < 4 else 2 * (8 - dz))
        n = min(n, nb - 1)
        dst = mq.at[n, qb, (y + 4 - (slab >> 2)) & 3, (x + 4 - (slab & 3)) & 3]
        if dz == 0:
            return pltpu.make_async_copy(stage.at[dz, qb], dst, sc_r.at[n, qb])
        return remote(stage.at[dz, qb], dst, sc_s.at[dz, qb], sc_r.at[n, qb], (slab, orb, aux))

    BLOCKS = [(dz, qb) for dz in (0, 1, 7, 2, 6) for qb in range(2)] + [(3, 0), (5, 1)]

    def pass_on():
        for dz, qb in BLOCKS:
            remote(stage.at[dz, qb], stage.at[dz, qb], sp_s.at[0, 0, qb], sp_r.at[dz, qb], sibling).wait_recv()
            behind(dz, qb).start()

    def sib_copy(n):
        mine = rows(c * 256, 256)
        part = pl.ds(n * 2, 2)
        return remote(mp.at[part, mine, :], mp.at[part, mine, :], sib_s.at[n], sib_r.at[n], sibling)

    for n in range(PARTS):
        sib_copy(n).start()

    keep = (z & 1)

    def e_copy():
        return remote(es.at[1 - keep], er, e_s, e_r, (zpair, orb, aux))

    def plane_copy(d):
        return remote(smy, sbuf.at[z, c, aux], pl_s.at[d - 1], pl_r.at[d - 1], (z, orb, (aux + d) & 7))


    def first_copy(part, way, d):
        span = pl.ds(part * 2, 2)
        piece = mq.at[span, way, el, i]
        peer = (x_peers if way == 0 else y_peers)[d]
        return remote(piece, piece, p1_s.at[part, way, d], p1_r.at[part, way, d], peer)

    def second_copy(part, way, d):
        span = pl.ds(part * 2, 2)
        piece = mq.at[span, 0, el] if way == 0 else mq.at[span, 1, :, i]
        peer = (y_peers if way == 0 else x_peers)[d]
        return remote(piece, piece, p2_s.at[part, way, d], p2_r.at[part, way, d], peer)

    def first(part):
        for n in (2 * part, 2 * part + 1):
            for qb in range(2):
                remote(mq.at[n, qb, 0, 0], mq.at[n, qb, 0, 0], sc_s.at[1, qb], sc_r.at[n, qb], sibling).wait_recv()
        for way in range(2):
            for d in range(3):
                first_copy(part, way, d).start()

    def second(part):
        for way in range(2):
            for d in range(3):
                first_copy(part, way, d).wait_recv()
            for d in range(3):
                second_copy(part, way, d).start()

    def second_done(part):
        for way in range(2):
            for d in range(3):
                second_copy(part, way, d).wait_recv()

        @pl.loop(part * 2, part * 2 + 2)
        def _(n):
            for qb in range(2):
                block = mq[n, qb].reshape(8, 2, 64, 128)
                for half in range(2):
                    mqt[n, qb * 128:(qb + 1) * 128, half * 512:(half + 1) * 512] = (
                        block[:, half].reshape(512, 128).T
                    )

    def z_copy(h, half, up):
        origin = (z + 8 - h) & 7 if up else (z + h) & 7
        piece = sbuf.at[origin, c, pl.ds(half * 4, 4)]
        way = 0 if up else 1
        return remote(piece, piece, z_s.at[way, half, h], z_r.at[way, half, h], z_next if up else z_last)

    def hops(half, up):
        return 4 if (half == 0) == up else 3

    def to_sibling(h, half, up):
        origin = (z + 8 - h) & 7 if up else (z + h) & 7
        piece = sbuf.at[origin, c, pl.ds(half * 4, 4)]
        way = 0 if up else 1
        return remote(piece, piece, t_s.at[way, half, h], t_r.at[way, half, h], sibling)

    WAYS = [(half, up) for half in range(2) for up in (True, False)]

    def z_event(h):
        for half, up in WAYS:
            if h <= hops(half, up):
                if h > 0:
                    z_copy(h - 1, half, up).wait_recv()
                if h < hops(half, up):
                    z_copy(h, half, up).start()
                if h > 0 or up:
                    to_sibling(h, half, up).start()

    def sibling_ready(h):
        for half, up in WAYS:
            if h <= hops(half, up) and (h > 0 or up):
                to_sibling(h, half, up).wait_recv()

    turn = 1 - 2 * ((z & 1))
    order = [(z >> 1), ((z >> 1) + 4 - turn) & 3, ((z >> 1) + 4 + turn) & 3, ((z >> 1) + 2) & 3]

    def o_copy(r, side):
        return remote(oout.at[r, side], oin.at[r, side], o_s.at[r, side], o_r.at[r, side], partner)

    def product(r, part):
        batches = slice(part * 2, part * 2 + 2)
        left = mqt[batches].reshape(512, 1024)
        for core in range(2):
            pair = sbuf[pl.ds(2 * order[r], 2), core].reshape(1024, 256)
            nt[:, :, core * 256:(core + 1) * 256] = (
                jnp.dot(left, pair, preferred_element_type=F32).astype(BF16).reshape(2, 256, 256)
            )
        for side in range(2):
            cols = slice(side * 256, (side + 1) * 256)
            total = jnp.dot(nt[0], mp[part * 2, :, cols], preferred_element_type=F32)
            total += jnp.dot(nt[1], mp[part * 2 + 1, :, cols], preferred_element_type=F32)
            total = total.reshape(2, 128, 256)
            if part > 0:
                total += own[r, side]
            own[r, side] = total
            if part == PARTS - 1:
                oout[r, side] = own[r, side, 1 - yh].astype(BF16)
                o_copy(r, side).start()

    def coefs(r):
        slot = slot_ref[order[r]]
        picked = []
        for j in range(4):
            total = jnp.zeros((8, 256), F32)
            for s in range(4):
                total = total + jnp.where(slot == s, table[j][s], 0.0)
            picked.append(total)
        return picked

    def add(r):
        picked = coefs(r)
        for side in range(2):
            o_copy(r, side).wait_recv()
            whole = (own[r, side, yh] + oin[r, side].astype(F32)).reshape(16, 8, 256)
            cols = slice(side * 256, (side + 1) * 256)
            for j in range(4):
                term = (picked[j] * whole).reshape(128, 256)
                if r == 0:
                    out_ref[j, :, cols] = term
                else:
                    out_ref[j, :, cols] += term

    load_g.wait()
    g_copy(0).wait_recv()
    es[...] = (0.5 * lax.dot_general(
        gc[...], g_in[...], (((1,), (1,)), ((), ())), preferred_element_type=F32
    )).reshape(2, 64, 256)
    e_copy().start()
    pass_on()

    e_copy().wait_recv()
    smy[...] = (es[keep] + er[...]).astype(BF16)
    for d in range(1, 8):
        plane_copy(d).start()
    sbuf[z, c, aux] = smy[...]
    for d in range(1, 8):
        plane_copy(d).wait_recv()
    z_event(0)
    first(0)
    first(1)
    first(2)
    second(0)
    z_event(1)
    second(1)
    z_event(2)
    second(2)
    table = [
        [cw_ref[j, s] * jnp.cos(jnp.full((8, 256), freq_ref[j] * time_ref[s], F32)) for s in range(4)]
        for j in range(4)
    ]
    for n in range(PARTS):
        sib_copy(n).wait_recv()
    sibling_ready(0)
    sibling_ready(1)
    second_done(0)
    product(0, 0)
    sibling_ready(2)
    product(1, 0)
    z_event(3)
    second_done(1)
    product(0, 1)
    product(1, 1)
    sibling_ready(3)
    product(2, 0)
    product(2, 1)
    z_event(4)
    sibling_ready(4)
    product(3, 0)
    product(3, 1)
    second_done(2)
    for r in range(4):
        product(r, 2)
    for r in range(4):
        add(r)

    @pl.when(c == (x >> 1))
    def _():
        for core in range(2):
            g_copy(core).wait_send()

    spread_all("wait")
    for dz, qb in BLOCKS:
        if dz > 0:
            behind(dz, qb).wait_send()
    for n in range(PARTS):
        sib_copy(n).wait_send()
        for way in range(2):
            for d in range(3):
                first_copy(n, way, d).wait_send()
                second_copy(n, way, d).wait_send()
    e_copy().wait_send()
    for d in range(1, 8):
        plane_copy(d).wait_send()
    for half, up in WAYS:
        for h in range(hops(half, up) + 1):
            if h < hops(half, up):
                z_copy(h, half, up).wait_send()
            if h > 0 or up:
                to_sibling(h, half, up).wait_send()
    for r in range(4):
        for side in range(2):
            o_copy(r, side).wait_send()


def per_device(
    three_center,
    block_mask,
    green_functions,
    time_slot,
    grid_times,
    grid_frequencies,
    cosine_weights,
):
    nb = three_center.shape[1]
    by_batch = jnp.transpose(three_center, (1, 0, 2))
    dma = pltpu.SemaphoreType.DMA
    vmem = pl.BlockSpec(memory_space=pltpu.VMEM)
    smem = pl.BlockSpec(memory_space=pltpu.SMEM)
    hbm = pl.BlockSpec(memory_space=pl.ANY)
    result = pl.pallas_call(
        kernel,
        name="polarizability",
        out_shape=jax.ShapeDtypeStruct((4, 128, 512), F32),
        in_specs=[hbm, hbm, smem, smem, smem, smem, smem],
        out_specs=vmem,
        scratch_shapes=[
            pltpu.VMEM((nb, 256, 512), BF16),
            pltpu.VMEM((256, 1024), BF16),
            pltpu.VMEM((nb, 512, 512), BF16),
            pltpu.VMEM((8, 2, 64, 128), BF16),
            pltpu.VMEM((nb, 2, 4, 4, 64, 128), BF16),
            pltpu.VMEM((nb, 256, 1024), BF16),
            pltpu.VMEM((8, 2, 8, 64, 256), BF16),
            pltpu.VMEM((128, 1024), BF16),
            pltpu.VMEM((2, 64, 256), F32),
            pltpu.VMEM((64, 256), F32),
            pltpu.VMEM((64, 256), BF16),
            pltpu.VMEM((2, 256, 512), BF16),
            pltpu.VMEM((4, 2, 2, 128, 256), F32),
            pltpu.VMEM((4, 2, 128, 256), BF16),
            pltpu.VMEM((4, 2, 128, 256), BF16),
            dma((2,)),
            dma((PARTS,)), dma((PARTS,)),
            dma((2,)), dma,
            dma, dma,
            dma((4, 2, 2)), dma((8, 2)),
            dma((8, 2)), dma((nb, 2)),
            dma((PARTS, 2, 3)), dma((PARTS, 2, 3)),
            dma((PARTS, 2, 3)), dma((PARTS, 2, 3)),
            dma((7,)), dma((7,)),
            dma((2, 2, 4)), dma((2, 2, 4)),
            dma((2, 2, 5)), dma((2, 2, 5)),
            dma((4, 2)), dma((4, 2)),
        ],
        compiler_params=pltpu.CompilerParams(
            collective_id=0, has_side_effects=True, vmem_limit_bytes=60 * 1024 * 1024
        ),
        cost_estimate=pl.CostEstimate(flops=9_700_000_000, bytes_accessed=3_000_000, transcendentals=0),
    )(
        by_batch, green_functions[0], jnp.transpose(block_mask, (0, 2, 1)),
        time_slot, grid_times, grid_frequencies, cosine_weights,
    )
    return jnp.transpose(result, (1, 0, 2))


def solution(mesh):
    return jax.shard_map(
        per_device,
        mesh=mesh,
        in_specs=(
            P("orb", None, "aux"),
            P("orb", None, "aux"),
            P("tm", "orb", None),
            P(),
            P(),
            P(),
            P(),
        ),
        out_specs=P(("tm", "orb"), None, "aux"),
        check_vma=False,
    )
```
